32 devices in a mesh: groups: 2 (over y), docs: 4 (over z), feat: 2 (over x), rep: 2 (over core).
Axes of the slice: x: 2, y: 2, z: 4, core: 2. Of those that a mesh axis runs over, the one named last changes fastest.
Arguments:
- activations: bfloat16 [8192, 8192], P(('groups', 'docs', 'rep'), 'feat'), parts along dimension 0, may hold values from -6 to 6
- out_grads: bfloat16 [8192, 8192], P(('groups', 'docs', 'rep'), 'feat'), parts along dimension 0, may hold values from -6 to 6
- proj_in: bfloat16 [8192, 128], P('feat'), may hold values from -0.0625 to 0.0625
- proj_out: bfloat16 [8192, 128], P('feat'), may hold values from -0.0625 to 0.0625
- inv_in: float32 [128, 128], replicated, may hold values from -0.5 to 2.5, as said below
- inv_out: float32 [128, 128], replicated, may hold values from -0.5 to 2.5, as said below
- segment_ids: int32 [8192], P(('groups', 'docs', 'rep')), parts along dimension 0, may hold values from 0 to 511, never falling along the last dimension, each value on 1 to 32 neighbouring positions
- owner_map: int32 [1024], P('groups'), parts along dimension 0, may hold values from 0 to 511
- stored: bfloat16 [4096, 16384], P(('groups', 'docs'), 'feat'), parts along dimension 0, may hold values from -0.005859375 to 0.005859375
Outputs:
- scores: float32 [1024, 2048], P(('groups', 'rep'), ('docs', 'feat')), parts along dimension 0
The draws below stay inside these ranges and needn't reach their ends.
There are 2 independent parts, one for each index of `groups`. The reference program is written for one: setup_inputs(seed, part) draws one part's arguments, and reference() takes and returns one part's arrays. A program takes and returns all parts, laid end to end along the dimension named above; an argument that names none is the same for every part. Nothing has to cross between parts.
Inputs may be any that keep to these rules, and one draw needn't show every extreme that they name: `inv_in`: symmetric. `inv_out`: symmetric. `segment_ids`: never falling along the tokens; each segment has 1 to 32 tokens, one exactly 32.
All inputs are finite; a program needn't handle non-finite values.
Results may differ from the reference program's by a relative error of at most 0.01.
Values may be sent and summed in bfloat16 or wider, within the bound.
A program may use at most 64 MiB of HBM per device.

```python
import math
import jax
import jax.numpy as jnp
import numpy as np
from jax import lax

D = 8192
R = 128
QUERIES = 512
TOK_DEV = 512
SEG_MOST = 32
TOKENS = 4096
SEGS = 512
DOCS = 2048
N_DOCS = 4
N_REP = 2


def curvature_factor(key):
    key_noise, key_scale = jax.random.split(key)
    noise = jax.random.normal(key_noise, (R, R), jnp.float32) * (0.3 / math.sqrt(R))
    diagonal = jnp.exp(jax.random.uniform(key_scale, (R,), jnp.float32, math.log(0.5), math.log(2.0)))
    return noise + noise.T + jnp.diag(diagonal)


def draw_inv_in(key, part):
    return curvature_factor(jax.random.fold_in(key, 11))


def draw_inv_out(key, part):
    return curvature_factor(jax.random.fold_in(key, 23))


def plant(entries, own_key, low, top_value):
    dims = entries.shape
    place = [jax.random.randint(jax.random.fold_in(own_key, axis), (), 0, dims[axis]) for axis in range(len(dims))]
    entries = entries.at[tuple(place)].set(low)
    longest = dims.index(max(dims))
    place[longest] = (place[longest] + 1) % dims[longest]
    return entries.at[tuple(place)].set(top_value)


def level_of(stream_key, extent, shards, least, high):
    def one(position, blocks):
        draws = jax.random.uniform(jax.random.fold_in(jax.random.fold_in(stream_key, 6), position), (blocks,), jnp.float32, least / len(shards), high / len(shards))
        return jnp.repeat(jnp.exp(draws), extent[position] // blocks).reshape((-1,) + (1,) * (len(extent) - position - 1))

    loudness = one(*shards[0])
    for cut in shards[1:]:
        loudness = loudness * one(*cut)
    return loudness


def split_up(number_of, total, reach, lean):
    portions = [(1 << 20) // math.isqrt(standing ** lean) + 1 for standing in range(2, number_of + 1)]
    surplus, given = total - reach - (number_of - 1), [1] * (number_of - 1)
    while surplus > 0:
        free = [i for i in range(number_of - 1) if given[i] < reach]
        pool, remaining = sum([portions[i] for i in free]), surplus
        for i in free:
            more = min(reach - given[i], max(1, remaining * portions[i] // pool), surplus)
            given[i] = given[i] + more
            surplus = surplus - more
    return np.array([reach] + given)


def ragged_sizes(key, amount, total, limit, lean):
    if amount == 2:
        one = jax.random.randint(key, (), max(1, total - limit), min(limit, total - 1) + 1)
        return jnp.stack([one, total - one])
    lengths = jnp.asarray(split_up(amount, total, limit, lean), jnp.int32)
    couples = (amount - 1) // 2
    giver, sink = lengths[1:1 + 2 * couples:2], lengths[2:2 + 2 * couples:2]
    margin = jnp.minimum(giver - 1, limit - sink)
    moved = jax.random.randint(jax.random.fold_in(key, 1), (couples,), 0, 1 << 20) % (margin + 1)
    lengths = lengths.at[1:1 + 2 * couples:2].set(giver - moved).at[2:2 + 2 * couples:2].set(sink + moved)
    return lengths[jax.random.permutation(jax.random.fold_in(key, 2), amount)]


def normal_values(own_key, dims, width, limit, cuts=(), kind=jnp.bfloat16):
    values = jax.random.normal(own_key, dims, jnp.float32) * width
    if len(cuts) > 0:
        values = level_of(own_key, dims, cuts, -0.22, 0.18) * values
    return jnp.clip(values, min=-limit, max=limit).astype(kind)


def setup_inputs(seed: int = 0, part: int = 0) -> dict:
    keys = jax.random.split(jax.random.key(seed), 10)
    part_splits = jax.random.split(jax.random.fold_in(keys[9], part), 10)
    return {
        "activations": normal_values(part_splits[0], (TOKENS, D), 1.0, 6.0, ((0, 8), (1, 2))),
        "out_grads": normal_values(part_splits[1], (TOKENS, D), 1.0, 6.0, ((0, 8), (1, 2))),
        "proj_in": normal_values(keys[2], (D, R), D ** -0.5, 0.0625, ((0, 2),)),
        "proj_out": normal_values(keys[3], (D, R), D ** -0.5, 0.0625, ((0, 2),)),
        "inv_in": draw_inv_in(jax.random.fold_in(keys[9], 71), part),
        "inv_out": draw_inv_out(jax.random.fold_in(keys[9], 71), part),
        "segment_ids": jnp.searchsorted(jnp.cumsum(ragged_sizes(part_splits[6], SEGS, TOKENS, SEG_MOST, 2)), jnp.arange(TOKENS), side="right").astype(jnp.int32),
        "owner_map": plant(jax.random.randint(part_splits[7], (SEGS,), 0, QUERIES), jax.random.fold_in(part_splits[7], 1), 0, QUERIES - 1).astype(jnp.int32),
        "stored": normal_values(part_splits[8], (DOCS, R * R), (R * R * 64) ** -0.5, 0.005859375, ((0, 4), (1, 2))),
    }


def reference(activations, out_grads, proj_in, proj_out, inv_in, inv_out, segment_ids, owner_map, stored):
    highest = lax.Precision.HIGHEST
    proj_x = jnp.dot(activations, proj_in, preferred_element_type=jnp.float32)
    proj_g = jnp.dot(out_grads, proj_out, preferred_element_type=jnp.float32)
    cond_x = jnp.dot(proj_x, inv_in, precision=highest, preferred_element_type=jnp.float32)
    cond_g = jnp.dot(proj_g, inv_out, precision=highest, preferred_element_type=jnp.float32)
    query = owner_map[segment_ids].astype(jnp.int32)
    shard_count = N_DOCS * N_REP
    block_x = cond_x.reshape(shard_count, TOK_DEV, R)
    block_g = cond_g.reshape(shard_count, TOK_DEV, R)
    block_q = query.reshape(shard_count, TOK_DEV)
    targets = jnp.arange(QUERIES, dtype=jnp.int32)

    def add_block(total, pieces):
        side_x, side_g, owners = pieces
        outer = (side_g[:, :, None] * side_x[:, None, :]).reshape(TOK_DEV, R * R).astype(jnp.bfloat16)
        onehot = (owners[:, None] == targets[None, :]).astype(jnp.float32)
        partial_value = lax.dot_general(onehot, outer.astype(jnp.float32), (((0,), (0,)), ((), ())), preferred_element_type=jnp.float32)
        rounded = lax.optimization_barrier(partial_value.astype(jnp.bfloat16))
        return total + rounded.astype(jnp.float32), None

    start_total = jnp.zeros((QUERIES, R * R), jnp.float32)
    total, unused = lax.scan(add_block, start_total, (block_x, block_g, block_q))
    features = total.astype(jnp.bfloat16)
    scores = lax.dot_general(features.astype(jnp.float32), stored.astype(jnp.float32), (((1,), (1,)), ((), ())), preferred_element_type=jnp.float32)
    return scores
```

```python
import functools
import jax
import jax.numpy as jnp
from jax import lax
from jax.experimental import pallas as pl
from jax.experimental.pallas import tpu as pltpu
from jax.sharding import PartitionSpec as P

QUERIES = 512
ROWS = 16
MESH = pl.DeviceIdType.MESH
F32, BF16 = jnp.float32, jnp.bfloat16


def flipped(me, step, count):
    if count & (count - 1):
        return lax.rem(me + step, count), lax.rem(me + count - step, count)
    other, bit = me, 1
    while bit < count:
        if step & bit:
            other = other + (1 - 2 * lax.rem(me // bit, 2)) * bit
        bit *= 2
    return other, other


def kernel(
    n_feat, n_docs, n_rep,
    act, grads, pin, pout, inv_in, inv_out, seg, owner, stored, out,
    act_v, grads_v, pin_v, pout_v, st_v,
    g_own, x_own, x_send, g_send, x_recv, g_recv, all_x, all_g, totals, acc,
    rep_recv, feat_send, feat_recv,
    load_sem, xs_sem, xr_sem, gs_sem, gr_sem, axs_sem, axr_sem, ags_sem, agr_sem,
    rs_sem, rr_sem, fs_sem, fr_sem,
):
    tokens = act.shape[0]
    width = inv_in.shape[0]
    side = width // n_feat
    half_tok = tokens // 2
    half_q = QUERIES // n_rep
    doc_rows = stored.shape[0] // n_feat
    feat, docs, rep = lax.axis_index("feat"), lax.axis_index("docs"), lax.axis_index("rep")

    def load(src, dst, index):
        return pltpu.make_async_copy(src, dst, load_sem.at[index])

    loads = [load(pin, pin_v, 0)]
    for i in range(2):
        rows = pl.ds(i * half_tok, half_tok)
        loads.append(load(act.at[rows], act_v.at[rows], 1 + i))
    loads.append(load(pout, pout_v, 3))
    for i in range(2):
        rows = pl.ds(i * half_tok, half_tok)
        loads.append(load(grads.at[rows], grads_v.at[rows], 4 + i))
    loads.append(load(stored, st_v, 6))
    for one in loads:
        one.start()

    barrier = pltpu.get_barrier_semaphore()
    feat_to = [flipped(feat, j, n_feat)[0] for j in range(n_feat)]
    docs_to = [flipped(docs, j, n_docs)[0] for j in range(n_docs)]
    rep_to = [flipped(rep, j, n_rep)[0] for j in range(n_rep)]
    for name, peers in (("feat", feat_to), ("docs", docs_to), ("rep", rep_to)):
        for peer in peers[1:]:
            pl.semaphore_signal(barrier, inc=1, device_id={name: peer}, device_id_type=MESH)

    seg_count = owner.shape[1]
    hit = lax.broadcasted_iota(jnp.int32, (seg_count, tokens), 0) == seg[...]
    hit = jnp.where(hit, 1.0, 0.0).astype(BF16)
    owners = owner[...]
    high = lax.div(owners, ROWS)
    low = owners - high * ROWS
    row = lax.broadcasted_iota(jnp.int32, (ROWS, seg_count), 0)
    digits = jnp.where(row == 0, high, jnp.where(row == 1, low, 0)).astype(F32).astype(BF16)
    all_g[0, side:, :] = jnp.dot(digits, hit, preferred_element_type=F32).astype(BF16)

    pl.semaphore_wait(barrier, (n_feat - 1) + (n_docs - 1) + (n_rep - 1))

    def send(src, dst, s_sem, r_sem, name, peer):
        return pltpu.make_async_remote_copy(
            src_ref=src, dst_ref=dst, send_sem=s_sem, recv_sem=r_sem,
            device_id={name: peer}, device_id_type=MESH,
        )

    def conditioned(values, proj_v, inv, first):
        parts = []
        for i in range(2):
            loads[first + i].wait()
            parts.append(jnp.dot(
                values[i * half_tok:(i + 1) * half_tok, :], proj_v[...], preferred_element_type=F32
            ))
        part = jnp.concatenate(parts, axis=0)
        return jnp.dot(
            part, inv[...], precision=lax.Precision.HIGHEST, preferred_element_type=F32
        ).T

    loads[0].wait()
    x_own[...] = conditioned(act_v, pin_v, inv_in, 1)
    x_send[...] = x_own[...].astype(BF16)
    x_copies, g_copies = [], []
    for j in range(1, n_feat):
        copy = send(x_send, x_recv.at[j], xs_sem.at[j], xr_sem.at[j], "feat", feat_to[j])
        copy.start()
        x_copies.append(copy)

    loads[3].wait()
    g_own[...] = conditioned(grads_v, pout_v, inv_out, 4)
    for j in range(1, n_feat):
        rows = pl.ds(pl.multiple_of(feat_to[j] * side, side), side)
        g_send[j] = g_own[rows, :].astype(BF16)
        copy = send(g_send.at[j], g_recv.at[j], gs_sem.at[j], gr_sem.at[j], "feat", feat_to[j])
        copy.start()
        g_copies.append(copy)

    x_sum = x_own[...]
    for j in range(1, n_feat):
        x_copies[j - 1].wait_recv()
        x_sum = x_sum + x_recv[j].astype(F32)
    all_x[0] = x_sum.astype(BF16)
    ax_copies, ag_copies = [], []
    for j in range(1, n_docs):
        copy = send(all_x.at[0], all_x.at[j], axs_sem.at[j], axr_sem.at[j], "docs", docs_to[j])
        copy.start()
        ax_copies.append(copy)
    g_sum = g_own[pl.ds(pl.multiple_of(feat * side, side), side), :]
    for j in range(1, n_feat):
        g_copies[j - 1].wait_recv()
        g_sum = g_sum + g_recv[j].astype(F32)
    all_g[0, :side, :] = g_sum.astype(BF16)
    for j in range(1, n_docs):
        copy = send(all_g.at[0], all_g.at[j], ags_sem.at[j], agr_sem.at[j], "docs", docs_to[j])
        copy.start()
        ag_copies.append(copy)

    loads[6].wait()
    acc[...] = jnp.zeros_like(acc)

    def shard(step, carry):
        @pl.when(step > 0)
        def _():
            send(all_x.at[0], all_x.at[step], axs_sem.at[step], axr_sem.at[step], "docs", docs_to[-1]).wait_recv()
            send(all_g.at[0], all_g.at[step], ags_sem.at[step], agr_sem.at[step], "docs", docs_to[-1]).wait_recv()

        totals[...] = jnp.zeros_like(totals)

        def chunk(c, inner):
            x = all_x[step].reshape(width // ROWS, ROWS, tokens)
            g = all_g[step, pl.ds(pl.multiple_of(c * ROWS, ROWS), ROWS), :].astype(F32)
            outer = []
            for j in range(ROWS):
                line = jnp.broadcast_to(g[j:j + 1, :], (ROWS, tokens)).astype(BF16)
                outer.append((x * line[None]).reshape(width, tokens))
            outer = jnp.concatenate(outer, axis=0)
            cols = pl.ds(pl.multiple_of(c * ROWS * width, ROWS * width), ROWS * width)
            totals[...] += jnp.dot(st_v[:, cols], outer, preferred_element_type=F32)
            return inner

        lax.fori_loop(0, side // ROWS, chunk, 0)
        digit = all_g[step, side:, :].astype(F32)
        query = (digit[0:1, :] * ROWS + digit[1:2, :]).astype(jnp.int32)
        mine = lax.broadcasted_iota(jnp.int32, (QUERIES, tokens), 0) == query
        mine = jnp.where(mine, 1.0, 0.0).astype(BF16)
        for f in range(n_feat):
            rows = totals[f * doc_rows:(f + 1) * doc_rows, :].astype(BF16)
            acc[f] += lax.dot_general(
                mine, rows, (((1,), (1,)), ((), ())), preferred_element_type=F32
            )
        return carry

    lax.fori_loop(0, n_docs, shard, 0)

    r_copies = []
    for j in range(1, n_rep):
        rows = pl.ds(pl.multiple_of(rep_to[j] * half_q, half_q), half_q)
        copy = send(acc.at[:, rows, :], rep_recv.at[j], rs_sem.at[j], rr_sem.at[j], "rep", rep_to[j])
        copy.start()
        r_copies.append(copy)
    for copy in r_copies:
        copy.wait_recv()
    own = pl.ds(pl.multiple_of(rep * half_q, half_q), half_q)

    def over_rep(f):
        value = acc[f, own, :]
        for j in range(1, n_rep):
            value = value + rep_recv[j, f]
        return value

    f_copies = []
    for j in range(1, n_feat):
        feat_send[j] = over_rep(feat_to[j]).astype(BF16)
        copy = send(feat_send.at[j], feat_recv.at[j], fs_sem.at[j], fr_sem.at[j], "feat", feat_to[j])
        copy.start()
        f_copies.append(copy)
    value = over_rep(feat)
    for j in range(1, n_feat):
        f_copies[j - 1].wait_recv()
        value = value + feat_recv[j].astype(F32)
    out[...] = value
    for copy in x_copies + g_copies + ax_copies + ag_copies + r_copies + f_copies:
        copy.wait_send()


def on_device(
    n_feat, n_docs, n_rep,
    activations, out_grads, proj_in, proj_out, inv_in, inv_out, segment_ids, owner_map, stored
):
    tokens = activations.shape[0]
    width = inv_in.shape[0]
    side = width // n_feat
    n_stored = stored.shape[0]
    doc_rows = n_stored // n_feat
    half_q = QUERIES // n_rep
    dma = pltpu.SemaphoreType.DMA
    anywhere = pl.BlockSpec(memory_space=pl.ANY)
    vmem = pl.BlockSpec(memory_space=pltpu.VMEM)
    return pl.pallas_call(
        functools.partial(kernel, n_feat, n_docs, n_rep),
        out_shape=jax.ShapeDtypeStruct((half_q, doc_rows), F32),
        in_specs=[anywhere] * 4 + [vmem] * 4 + [anywhere],
        out_specs=vmem,
        scratch_shapes=[
            pltpu.VMEM(activations.shape, BF16),
            pltpu.VMEM(out_grads.shape, BF16),
            pltpu.VMEM(proj_in.shape, BF16),
            pltpu.VMEM(proj_out.shape, BF16),
            pltpu.VMEM(stored.shape, BF16),
            pltpu.VMEM((width, tokens), F32),
            pltpu.VMEM((width, tokens), F32),
            pltpu.VMEM((width, tokens), BF16),
            pltpu.VMEM((n_feat, side, tokens), BF16),
            pltpu.VMEM((n_feat, width, tokens), BF16),
            pltpu.VMEM((n_feat, side, tokens), BF16),
            pltpu.VMEM((n_docs, width, tokens), BF16),
            pltpu.VMEM((n_docs, side + ROWS, tokens), BF16),
            pltpu.VMEM((n_stored, tokens), F32),
            pltpu.VMEM((n_feat, QUERIES, doc_rows), F32),
            pltpu.VMEM((n_rep, n_feat, half_q, doc_rows), F32),
            pltpu.VMEM((n_feat, half_q, doc_rows), BF16),
            pltpu.VMEM((n_feat, half_q, doc_rows), BF16),
            dma((7,)),
            dma((n_feat,)), dma((n_feat,)), dma((n_feat,)), dma((n_feat,)),
            dma((n_docs,)), dma((n_docs,)), dma((n_docs,)), dma((n_docs,)),
            dma((n_rep,)), dma((n_rep,)), dma((n_feat,)), dma((n_feat,)),
        ],
        compiler_params=pltpu.CompilerParams(
            collective_id=0, has_side_effects=True, vmem_limit_bytes=56 * 1024 * 1024
        ),
    )(
        activations, out_grads, proj_in, proj_out, inv_in, inv_out,
        segment_ids.reshape(1, -1), owner_map.reshape(1, -1), stored,
    )


def solution(mesh):
    placed = (
        P(("groups", "docs", "rep"), "feat"),
        P(("groups", "docs", "rep"), "feat"),
        P("feat", None),
        P("feat", None),
        P(),
        P(),
        P(("groups", "docs", "rep")),
        P("groups"),
        P(("groups", "docs"), "feat"),
    )
    sizes = dict(mesh.shape)
    return jax.shard_map(
        functools.partial(on_device, sizes["feat"], sizes["docs"], sizes["rep"]),
        mesh=mesh,
        in_specs=placed,
        out_specs=P(("groups", "rep"), ("docs", "feat")),
        check_vma=False,
    )
```

```python
import functools
import jax
import jax.numpy as jnp
from jax import lax
from jax.experimental import pallas as pl
from jax.experimental.pallas import tpu as pltpu
from jax.sharding import PartitionSpec as P

QUERIES = 512
ROWS = 16
MESH = pl.DeviceIdType.MESH
F32, BF16 = jnp.float32, jnp.bfloat16


def flipped(me, step, count):
    if count & (count - 1):
        return lax.rem(me + step, count), lax.rem(me + count - step, count)
    other, bit = me, 1
    while bit < count:
        if step & bit:
            other = other + (1 - 2 * lax.rem(me // bit, 2)) * bit
        bit *= 2
    return other, other


def kernel(
    n_feat, n_docs, n_rep,
    act, grads, pin, pout, inv_in, inv_out, seg, owner, stored, out,
    act_v, grads_v, pin_v, pout_v, st_v,
    g_own, x_own, x_send, g_send, x_recv, g_recv, all_x, all_g, totals, acc,
    rep_recv, feat_send, feat_recv,
    load_sem, xs_sem, xr_sem, gs_sem, gr_sem, axs_sem, axr_sem, ags_sem, agr_sem,
    rs_sem, rr_sem, fs_sem, fr_sem, bs_sem, br_sem,
):
    tokens = act.shape[0]
    width = inv_in.shape[0]
    side = width // n_feat
    half_tok = tokens // 2
    half_q = QUERIES // n_rep
    doc_rows = stored.shape[0] // n_feat
    feat, docs, rep = lax.axis_index("feat"), lax.axis_index("docs"), lax.axis_index("rep")

    def load(src, dst, index):
        return pltpu.make_async_copy(src, dst, load_sem.at[index])

    loads = [load(pin, pin_v, 0)]
    for i in range(2):
        rows = pl.ds(i * half_tok, half_tok)
        loads.append(load(act.at[rows], act_v.at[rows], 1 + i))
    loads.append(load(pout, pout_v, 3))
    for i in range(2):
        rows = pl.ds(i * half_tok, half_tok)
        loads.append(load(grads.at[rows], grads_v.at[rows], 4 + i))
    loads.append(load(stored, st_v, 6))
    for one in loads:
        one.start()

    barrier = pltpu.get_barrier_semaphore()
    feat_to = [flipped(feat, j, n_feat)[0] for j in range(n_feat)]
    docs_to = [flipped(docs, j, n_docs)[0] for j in range(n_docs)]
    rep_to = [flipped(rep, j, n_rep)[0] for j in range(n_rep)]
    for name, peers in (("feat", feat_to), ("docs", docs_to), ("rep", rep_to)):
        for peer in peers[1:]:
            pl.semaphore_signal(barrier, inc=1, device_id={name: peer}, device_id_type=MESH)

    seg_count = owner.shape[1]
    hit = lax.broadcasted_iota(jnp.int32, (seg_count, tokens), 0) == seg[...]
    hit = jnp.where(hit, 1.0, 0.0).astype(BF16)
    owners = owner[...]
    high = lax.div(owners, ROWS)
    low = owners - high * ROWS
    row = lax.broadcasted_iota(jnp.int32, (ROWS, seg_count), 0)
    digits = jnp.where(row == 0, high, jnp.where(row == 1, low, 0)).astype(F32).astype(BF16)
    all_g[0, side:, :] = jnp.dot(digits, hit, preferred_element_type=F32).astype(BF16)

    pl.semaphore_wait(barrier, (n_feat - 1) + (n_docs - 1) + (n_rep - 1))

    def send(src, dst, s_sem, r_sem, name, peer):
        return pltpu.make_async_remote_copy(
            src_ref=src, dst_ref=dst, send_sem=s_sem, recv_sem=r_sem,
            device_id={name: peer}, device_id_type=MESH,
        )

    def conditioned(values, proj_v, inv, first):
        parts = []
        for i in range(2):
            loads[first + i].wait()
            parts.append(jnp.dot(
                values[i * half_tok:(i + 1) * half_tok, :], proj_v[...], preferred_element_type=F32
            ))
        part = jnp.concatenate(parts, axis=0)
        return jnp.dot(
            part, inv[...], precision=lax.Precision.HIGHEST, preferred_element_type=F32
        ).T

    loads[0].wait()
    x_own[...] = conditioned(act_v, pin_v, inv_in, 1)
    x_copies, g_copies = [], []
    for j in range(1, n_feat):
        rows = pl.ds(pl.multiple_of(feat_to[j] * side, side), side)
        x_send[j] = x_own[rows, :].astype(BF16)
        copy = send(x_send.at[j], x_recv.at[j], xs_sem.at[j], xr_sem.at[j], "feat", feat_to[j])
        copy.start()
        x_copies.append(copy)

    loads[3].wait()
    g_own[...] = conditioned(grads_v, pout_v, inv_out, 4)
    for j in range(1, n_feat):
        rows = pl.ds(pl.multiple_of(feat_to[j] * side, side), side)
        g_send[j] = g_own[rows, :].astype(BF16)
        copy = send(g_send.at[j], g_recv.at[j], gs_sem.at[j], gr_sem.at[j], "feat", feat_to[j])
        copy.start()
        g_copies.append(copy)

    my_rows = pl.ds(pl.multiple_of(feat * side, side), side)

    def share(step, j):
        part = all_x.at[step, my_rows]
        return send(part, part, bs_sem.at[step, j], br_sem.at[step, j], "feat", feat_to[j])

    x_sum = x_own[my_rows, :]
    for j in range(1, n_feat):
        x_copies[j - 1].wait_recv()
        x_sum = x_sum + x_recv[j].astype(F32)
    all_x[0, my_rows, :] = x_sum.astype(BF16)
    ax_copies, ag_copies = [], []
    for j in range(1, n_docs):
        part = (all_x.at[0, my_rows], all_x.at[j, my_rows])
        copy = send(*part, axs_sem.at[j], axr_sem.at[j], "docs", docs_to[j])
        copy.start()
        ax_copies.append(copy)
    for j in range(1, n_feat):
        share(0, j).start()
    g_sum = g_own[my_rows, :]
    for j in range(1, n_feat):
        g_copies[j - 1].wait_recv()
        g_sum = g_sum + g_recv[j].astype(F32)
    all_g[0, :side, :] = g_sum.astype(BF16)
    for j in range(1, n_docs):
        copy = send(all_g.at[0], all_g.at[j], ags_sem.at[j], agr_sem.at[j], "docs", docs_to[j])
        copy.start()
        ag_copies.append(copy)

    loads[6].wait()
    acc[...] = jnp.zeros_like(acc)

    def shard(step, carry):
        for j in range(1, n_feat):
            share(step, j).wait()

        @pl.when(step > 0)
        def _():
            send(all_g.at[0], all_g.at[step], ags_sem.at[step], agr_sem.at[step], "docs", docs_to[-1]).wait_recv()

        totals[...] = jnp.zeros_like(totals)

        def chunk(c, inner):
            x = all_x[step].reshape(width // ROWS, ROWS, tokens)
            g = all_g[step, pl.ds(pl.multiple_of(c * ROWS, ROWS), ROWS), :].astype(F32)
            outer = []
            for j in range(ROWS):
                line = jnp.broadcast_to(g[j:j + 1, :], (ROWS, tokens)).astype(BF16)
                outer.append((x * line[None]).reshape(width, tokens))
            outer = jnp.concatenate(outer, axis=0)
            cols = pl.ds(pl.multiple_of(c * ROWS * width, ROWS * width), ROWS * width)
            totals[...] += jnp.dot(st_v[:, cols], outer, preferred_element_type=F32)
            return inner

        chunks = side // ROWS
        lax.fori_loop(0, chunks // 2, chunk, 0)

        @pl.when(step + 1 < n_docs)
        def _():
            part = (all_x.at[0, my_rows], all_x.at[step + 1, my_rows])
            send(*part, axs_sem.at[step + 1], axr_sem.at[step + 1], "docs", docs_to[-1]).wait_recv()
            for j in range(1, n_feat):
                share(step + 1, j).start()

        lax.fori_loop(chunks // 2, chunks, chunk, 0)
        digit = all_g[step, side:, :].astype(F32)
        query = (digit[0:1, :] * ROWS + digit[1:2, :]).astype(jnp.int32)
        mine = lax.broadcasted_iota(jnp.int32, (QUERIES, tokens), 0) == query
        mine = jnp.where(mine, 1.0, 0.0).astype(BF16)
        for f in range(n_feat):
            rows = totals[f * doc_rows:(f + 1) * doc_rows, :].astype(BF16)
            acc[f] += lax.dot_general(
                mine, rows, (((1,), (1,)), ((), ())), preferred_element_type=F32
            )
        return carry

    lax.fori_loop(0, n_docs, shard, 0)

    r_copies = []
    for j in range(1, n_rep):
        rows = pl.ds(pl.multiple_of(rep_to[j] * half_q, half_q), half_q)
        copy = send(acc.at[:, rows, :], rep_recv.at[j], rs_sem.at[j], rr_sem.at[j], "rep", rep_to[j])
        copy.start()
        r_copies.append(copy)
    for copy in r_copies:
        copy.wait_recv()
    own = pl.ds(pl.multiple_of(rep * half_q, half_q), half_q)

    def over_rep(f):
        value = acc[f, own, :]
        for j in range(1, n_rep):
            value = value + rep_recv[j, f]
        return value

    f_copies = []
    for j in range(1, n_feat):
        feat_send[j] = over_rep(feat_to[j]).astype(BF16)
        copy = send(feat_send.at[j], feat_recv.at[j], fs_sem.at[j], fr_sem.at[j], "feat", feat_to[j])
        copy.start()
        f_copies.append(copy)
    value = over_rep(feat)
    for j in range(1, n_feat):
        f_copies[j - 1].wait_recv()
        value = value + feat_recv[j].astype(F32)
    out[...] = value
    for copy in x_copies + g_copies + ax_copies + ag_copies + r_copies + f_copies:
        copy.wait_send()


def on_device(
    n_feat, n_docs, n_rep,
    activations, out_grads, proj_in, proj_out, inv_in, inv_out, segment_ids, owner_map, stored
):
    tokens = activations.shape[0]
    width = inv_in.shape[0]
    side = width // n_feat
    n_stored = stored.shape[0]
    doc_rows = n_stored // n_feat
    half_q = QUERIES // n_rep
    dma = pltpu.SemaphoreType.DMA
    anywhere = pl.BlockSpec(memory_space=pl.ANY)
    vmem = pl.BlockSpec(memory_space=pltpu.VMEM)
    return pl.pallas_call(
        functools.partial(kernel, n_feat, n_docs, n_rep),
        out_shape=jax.ShapeDtypeStruct((half_q, doc_rows), F32),
        in_specs=[anywhere] * 4 + [vmem] * 4 + [anywhere],
        out_specs=vmem,
        scratch_shapes=[
            pltpu.VMEM(activations.shape, BF16),
            pltpu.VMEM(out_grads.shape, BF16),
            pltpu.VMEM(proj_in.shape, BF16),
            pltpu.VMEM(proj_out.shape, BF16),
            pltpu.VMEM(stored.shape, BF16),
            pltpu.VMEM((width, tokens), F32),
            pltpu.VMEM((width, tokens), F32),
            pltpu.VMEM((n_feat, side, tokens), BF16),
            pltpu.VMEM((n_feat, side, tokens), BF16),
            pltpu.VMEM((n_feat, side, tokens), BF16),
            pltpu.VMEM((n_feat, side, tokens), BF16),
            pltpu.VMEM((n_docs, width, tokens), BF16),
            pltpu.VMEM((n_docs, side + ROWS, tokens), BF16),
            pltpu.VMEM((n_stored, tokens), F32),
            pltpu.VMEM((n_feat, QUERIES, doc_rows), F32),
            pltpu.VMEM((n_rep, n_feat, half_q, doc_rows), F32),
            pltpu.VMEM((n_feat, half_q, doc_rows), BF16),
            pltpu.VMEM((n_feat, half_q, doc_rows), BF16),
            dma((7,)),
            dma((n_feat,)), dma((n_feat,)), dma((n_feat,)), dma((n_feat,)),
            dma((n_docs,)), dma((n_docs,)), dma((n_docs,)), dma((n_docs,)),
            dma((n_rep,)), dma((n_rep,)), dma((n_feat,)), dma((n_feat,)),
            dma((n_docs, n_feat)), dma((n_docs, n_feat)),
        ],
        compiler_params=pltpu.CompilerParams(
            collective_id=0, has_side_effects=True, vmem_limit_bytes=56 * 1024 * 1024
        ),
    )(
        activations, out_grads, proj_in, proj_out, inv_in, inv_out,
        segment_ids.reshape(1, -1), owner_map.reshape(1, -1), stored,
    )


def solution(mesh):
    placed = (
        P(("groups", "docs", "rep"), "feat"),
        P(("groups", "docs", "rep"), "feat"),
        P("feat", None),
        P("feat", None),
        P(),
        P(),
        P(("groups", "docs", "rep")),
        P("groups"),
        P(("groups", "docs"), "feat"),
    )
    sizes = dict(mesh.shape)
    return jax.shard_map(
        functools.partial(on_device, sizes["feat"], sizes["docs"], sizes["rep"]),
        mesh=mesh,
        in_specs=placed,
        out_specs=P(("groups", "rep"), ("docs", "feat")),
        check_vma=False,
    )
```

```python
import functools
import jax
import jax.numpy as jnp
from jax import lax
from jax.experimental import pallas as pl
from jax.experimental.pallas import tpu as pltpu
from jax.sharding import PartitionSpec as P

QUERIES = 512
ROWS = 16
CUTS = 4
MESH = pl.DeviceIdType.MESH
F32, BF16 = jnp.float32, jnp.bfloat16


def flipped(me, step, count):
    if count & (count - 1):
        return lax.rem(me + step, count), lax.rem(me + count - step, count)
    other, bit = me, 1
    while bit < count:
        if step & bit:
            other = other + (1 - 2 * lax.rem(me // bit, 2)) * bit
        bit *= 2
    return other, other


def kernel(
    n_feat, n_docs, n_rep,
    act, grads, pin, pout, inv_in, inv_out, seg, owner, stored, out,
    act_v, grads_v, pin_v, pout_v, st_v,
    g_own, x_own, x_send, g_send, x_recv, g_recv, all_x, all_g, totals, acc,
    rep_recv, feat_send, feat_recv,
    load_sem, xs_sem, xr_sem, gs_sem, gr_sem, axs_sem, axr_sem, ags_sem, agr_sem,
    rs_sem, rr_sem, fs_sem, fr_sem, bs_sem, br_sem,
):
    tokens = act.shape[0]
    width = inv_in.shape[0]
    side = width // n_feat
    cut = act.shape[1] // CUTS
    half_q = QUERIES // n_rep
    doc_rows = stored.shape[0] // n_feat
    feat, docs, rep = lax.axis_index("feat"), lax.axis_index("docs"), lax.axis_index("rep")

    def load(src, dst, index):
        return pltpu.make_async_copy(src, dst, load_sem.at[index])

    loads = [load(pin, pin_v, 0)]
    for i in range(CUTS):
        cols = pl.ds(i * cut, cut)
        loads.append(load(act.at[:, cols], act_v.at[:, cols], 1 + i))
    loads.append(load(pout, pout_v, 1 + CUTS))
    for i in range(CUTS):
        cols = pl.ds(i * cut, cut)
        loads.append(load(grads.at[:, cols], grads_v.at[:, cols], 2 + CUTS + i))
    loads.append(load(stored, st_v, 2 + 2 * CUTS))
    for one in loads:
        one.start()

    barrier = pltpu.get_barrier_semaphore()
    feat_to = [flipped(feat, j, n_feat)[0] for j in range(n_feat)]
    docs_to = [flipped(docs, j, n_docs)[0] for j in range(n_docs)]
    rep_to = [flipped(rep, j, n_rep)[0] for j in range(n_rep)]
    for name, peers in (("feat", feat_to), ("docs", docs_to), ("rep", rep_to)):
        for peer in peers[1:]:
            pl.semaphore_signal(barrier, inc=1, device_id={name: peer}, device_id_type=MESH)

    seg_count = owner.shape[1]
    hit = lax.broadcasted_iota(jnp.int32, (seg_count, tokens), 0) == seg[...]
    hit = jnp.where(hit, 1.0, 0.0).astype(BF16)
    owners = owner[...]
    high = lax.div(owners, ROWS)
    low = owners - high * ROWS
    row = lax.broadcasted_iota(jnp.int32, (ROWS, seg_count), 0)
    digits = jnp.where(row == 0, high, jnp.where(row == 1, low, 0)).astype(F32).astype(BF16)
    all_g[0, side:, :] = jnp.dot(digits, hit, preferred_element_type=F32).astype(BF16)

    def send(src, dst, s_sem, r_sem, name, peer):
        return pltpu.make_async_remote_copy(
            src_ref=src, dst_ref=dst, send_sem=s_sem, recv_sem=r_sem,
            device_id={name: peer}, device_id_type=MESH,
        )

    def conditioned(values, proj_v, inv, first):
        part = None
        for i in range(CUTS):
            loads[first + i].wait()
            cols = slice(i * cut, (i + 1) * cut)
            more = jnp.dot(values[:, cols], proj_v[cols, :], preferred_element_type=F32)
            part = more if part is None else part + more
        return jnp.dot(
            part, inv[...], precision=lax.Precision.HIGHEST, preferred_element_type=F32
        ).T

    loads[0].wait()
    x_own[...] = conditioned(act_v, pin_v, inv_in, 1)
    pl.semaphore_wait(barrier, (n_feat - 1) + (n_docs - 1) + (n_rep - 1))
    x_copies, g_copies = [], []
    for j in range(1, n_feat):
        rows = pl.ds(pl.multiple_of(feat_to[j] * side, side), side)
        x_send[j] = x_own[rows, :].astype(BF16)
        copy = send(x_send.at[j], x_recv.at[j], xs_sem.at[j], xr_sem.at[j], "feat", feat_to[j])
        copy.start()
        x_copies.append(copy)

    loads[1 + CUTS].wait()
    g_own[...] = conditioned(grads_v, pout_v, inv_out, 2 + CUTS)
    for j in range(1, n_feat):
        rows = pl.ds(pl.multiple_of(feat_to[j] * side, side), side)
        g_send[j] = g_own[rows, :].astype(BF16)
        copy = send(g_send.at[j], g_recv.at[j], gs_sem.at[j], gr_sem.at[j], "feat", feat_to[j])
        copy.start()
        g_copies.append(copy)

    my_rows = pl.ds(pl.multiple_of(feat * side, side), side)

    def share(step, j):
        part = all_x.at[step, my_rows]
        return send(part, part, bs_sem.at[step, j], br_sem.at[step, j], "feat", feat_to[j])

    x_sum = x_own[my_rows, :]
    for j in range(1, n_feat):
        x_copies[j - 1].wait_recv()
        x_sum = x_sum + x_recv[j].astype(F32)
    all_x[0, my_rows, :] = x_sum.astype(BF16)
    ax_copies, ag_copies = [], []
    for j in range(1, n_docs):
        part = (all_x.at[0, my_rows], all_x.at[j, my_rows])
        copy = send(*part, axs_sem.at[j], axr_sem.at[j], "docs", docs_to[j])
        copy.start()
        ax_copies.append(copy)
    for j in range(1, n_feat):
        share(0, j).start()
    g_sum = g_own[my_rows, :]
    for j in range(1, n_feat):
        g_copies[j - 1].wait_recv()
        g_sum = g_sum + g_recv[j].astype(F32)
    all_g[0, :side, :] = g_sum.astype(BF16)
    for j in range(1, n_docs):
        copy = send(all_g.at[0], all_g.at[j], ags_sem.at[j], agr_sem.at[j], "docs", docs_to[j])
        copy.start()
        ag_copies.append(copy)

    loads[2 + 2 * CUTS].wait()
    acc[...] = jnp.zeros_like(acc)

    chunks = side // ROWS

    def arrive(step):
        for j in range(1, n_feat):
            share(step, j).wait()

        @pl.when(step > 0)
        def _():
            send(all_g.at[0], all_g.at[step], ags_sem.at[step], agr_sem.at[step], "docs", docs_to[-1]).wait_recv()

    def forward(step):
        part = (all_x.at[0, my_rows], all_x.at[step, my_rows])
        send(*part, axs_sem.at[step], axr_sem.at[step], "docs", docs_to[-1]).wait_recv()
        for j in range(1, n_feat):
            share(step, j).start()

    def multiply(step, rows, first, last):
        def chunk(c, inner):
            x = all_x[step].reshape(width // ROWS, ROWS, tokens)
            g = all_g[step, pl.ds(pl.multiple_of(c * ROWS, ROWS), ROWS), :].astype(F32)
            outer = []
            for j in range(ROWS):
                line = jnp.broadcast_to(g[j:j + 1, :], (ROWS, tokens)).astype(BF16)
                outer.append((x * line[None]).reshape(width, tokens))
            outer = jnp.concatenate(outer, axis=0)
            cols = pl.ds(pl.multiple_of(c * ROWS * width, ROWS * width), ROWS * width)
            totals[rows, :] += jnp.dot(st_v[rows, cols], outer, preferred_element_type=F32)
            return inner

        lax.fori_loop(first, last, chunk, 0)

    def owned(step):
        digit = all_g[step, side:, :].astype(F32)
        query = (digit[0:1, :] * ROWS + digit[1:2, :]).astype(jnp.int32)
        mine = lax.broadcasted_iota(jnp.int32, (QUERIES, tokens), 0) == query
        return jnp.where(mine, 1.0, 0.0).astype(BF16)

    def gather(mine, f, rows):
        acc[f] += lax.dot_general(
            mine, totals[rows, :].astype(BF16), (((1,), (1,)), ((), ())),
            preferred_element_type=F32,
        )

    def shard(step, carry):
        arrive(step)
        totals[...] = jnp.zeros_like(totals)
        whole = pl.ds(0, n_feat * doc_rows)
        multiply(step, whole, 0, chunks // 2)
        forward(step + 1)
        multiply(step, whole, chunks // 2, chunks)
        mine = owned(step)
        for f in range(n_feat):
            gather(mine, f, pl.ds(f * doc_rows, doc_rows))
        return carry

    lax.fori_loop(0, n_docs - 2, shard, 0)

    def slice_of(step, i, fresh):
        rows = pl.ds(pl.multiple_of(feat_to[i] * doc_rows, doc_rows), doc_rows)
        totals[rows, :] = jnp.zeros((doc_rows, tokens), F32)
        if fresh:
            arrive(step)
        multiply(step, rows, 0, chunks // 2)
        if fresh and step + 1 < n_docs:
            forward(step + 1)
        multiply(step, rows, chunks // 2, chunks)
        gather(owned(step), feat_to[i], rows)

    r_copies, f_copies = [], []

    def to_rep(i):
        for j in range(1, n_rep):
            rows = pl.ds(pl.multiple_of(rep_to[j] * half_q, half_q), half_q)
            part = (acc.at[feat_to[i], rows], rep_recv.at[j, feat_to[i]])
            copy = send(*part, rs_sem.at[j, i], rr_sem.at[j, i], "rep", rep_to[j])
            copy.start()
            r_copies.append((i, copy))

    own = pl.ds(pl.multiple_of(rep * half_q, half_q), half_q)

    def over_rep(i):
        for at, copy in r_copies:
            if at == i:
                copy.wait_recv()
        value = acc[feat_to[i], own, :]
        for j in range(1, n_rep):
            value = value + rep_recv[j, feat_to[i]]
        return value

    for i in range(1, n_feat):
        for step in range(n_docs - 2, n_docs):
            slice_of(step, i, i == 1)
        to_rep(i)
    slice_of(n_docs - 2, 0, False)
    for j in range(1, n_feat):
        feat_send[j] = over_rep(j).astype(BF16)
        copy = send(feat_send.at[j], feat_recv.at[j], fs_sem.at[j], fr_sem.at[j], "feat", feat_to[j])
        copy.start()
        f_copies.append(copy)
    slice_of(n_docs - 1, 0, False)
    to_rep(0)
    value = over_rep(0)
    for j in range(1, n_feat):
        f_copies[j - 1].wait_recv()
        value = value + feat_recv[j].astype(F32)
    out[...] = value
    for copy in x_copies + g_copies + ax_copies + ag_copies + [c for _, c in r_copies] + f_copies:
        copy.wait_send()


def on_device(
    n_feat, n_docs, n_rep,
    activations, out_grads, proj_in, proj_out, inv_in, inv_out, segment_ids, owner_map, stored
):
    tokens = activations.shape[0]
    width = inv_in.shape[0]
    side = width // n_feat
    n_stored = stored.shape[0]
    doc_rows = n_stored // n_feat
    half_q = QUERIES // n_rep
    dma = pltpu.SemaphoreType.DMA
    anywhere = pl.BlockSpec(memory_space=pl.ANY)
    vmem = pl.BlockSpec(memory_space=pltpu.VMEM)
    return pl.pallas_call(
        functools.partial(kernel, n_feat, n_docs, n_rep),
        out_shape=jax.ShapeDtypeStruct((half_q, doc_rows), F32),
        in_specs=[anywhere] * 4 + [vmem] * 4 + [anywhere],
        out_specs=vmem,
        scratch_shapes=[
            pltpu.VMEM(activations.shape, BF16),
            pltpu.VMEM(out_grads.shape, BF16),
            pltpu.VMEM(proj_in.shape, BF16),
            pltpu.VMEM(proj_out.shape, BF16),
            pltpu.VMEM(stored.shape, BF16),
            pltpu.VMEM((width, tokens), F32),
            pltpu.VMEM((width, tokens), F32),
            pltpu.VMEM((n_feat, side, tokens), BF16),
            pltpu.VMEM((n_feat, side, tokens), BF16),
            pltpu.VMEM((n_feat, side, tokens), BF16),
            pltpu.VMEM((n_feat, side, tokens), BF16),
            pltpu.VMEM((n_docs, width, tokens), BF16),
            pltpu.VMEM((n_docs, side + ROWS, tokens), BF16),
            pltpu.VMEM((n_stored, tokens), F32),
            pltpu.VMEM((n_feat, QUERIES, doc_rows), F32),
            pltpu.VMEM((n_rep, n_feat, half_q, doc_rows), F32),
            pltpu.VMEM((n_feat, half_q, doc_rows), BF16),
            pltpu.VMEM((n_feat, half_q, doc_rows), BF16),
            dma((3 + 2 * CUTS,)),
            dma((n_feat,)), dma((n_feat,)), dma((n_feat,)), dma((n_feat,)),
            dma((n_docs,)), dma((n_docs,)), dma((n_docs,)), dma((n_docs,)),
            dma((n_rep, n_feat)), dma((n_rep, n_feat)), dma((n_feat,)), dma((n_feat,)),
            dma((n_docs, n_feat)), dma((n_docs, n_feat)),
        ],
        compiler_params=pltpu.CompilerParams(
            collective_id=0, has_side_effects=True, vmem_limit_bytes=56 * 1024 * 1024
        ),
    )(
        activations, out_grads, proj_in, proj_out, inv_in, inv_out,
        segment_ids.reshape(1, -1), owner_map.reshape(1, -1), stored,
    )


def solution(mesh):
    placed = (
        P(("groups", "docs", "rep"), "feat"),
        P(("groups", "docs", "rep"), "feat"),
        P("feat", None),
        P("feat", None),
        P(),
        P(),
        P(("groups", "docs", "rep")),
        P("groups"),
        P(("groups", "docs"), "feat"),
    )
    sizes = dict(mesh.shape)
    return jax.shard_map(
        functools.partial(on_device, sizes["feat"], sizes["docs"], sizes["rep"]),
        mesh=mesh,
        in_specs=placed,
        out_specs=P(("groups", "rep"), ("docs", "feat")),
        check_vma=False,
    )
```
